32 devices in a mesh: groups: 2 (over x), win: 8 (over z, y), gx: 2 (over core).
Axes of the slice: x: 2, y: 2, z: 4, core: 2. Of those that a mesh axis runs over, the one named last changes fastest.
Arguments:
- prev_states: float32 [16, 1024, 128], P(('groups', 'win'), 'gx'), parts along dimension 0, may hold values from -6 to 6
- timesteps: int32 [16], P(('groups', 'win')), parts along dimension 0, may hold values from 0 to 999
- step_sizes: float32 [16], P(('groups', 'win')), parts along dimension 0, may hold values from 0.1 to 0.3
- slide: int32 [1], replicated, may hold values from 1 to 8
- w_time: bfloat16 [256, 768], replicated, may hold values from -0.375 to 0.375
- w_ada: bfloat16 [1, 768, 4608], replicated, may hold values from -0.21875 to 0.21875
- w_in: bfloat16 [128, 768], replicated, may hold values from -0.5 to 0.5
- w_qkv: bfloat16 [1, 768, 2304], replicated, may hold values from -2 to 2
- w_proj: bfloat16 [1, 768, 768], replicated, may hold values from -0.21875 to 0.21875
- w_up: bfloat16 [1, 768, 3072], replicated, may hold values from -0.21875 to 0.21875
- w_down: bfloat16 [1, 3072, 768], replicated, may hold values from -0.109375 to 0.109375
- w_out: bfloat16 [768, 128], replicated, may hold values from -0.21875 to 0.21875
Outputs:
- states_out: float32 [16, 1024, 128], P(('groups', 'win'), 'gx'), parts along dimension 0
The draws below stay inside these ranges and needn't reach their ends.
There are 2 independent parts, one for each index of `groups`. The reference program is written for one: setup_inputs(seed, part) draws one part's arguments, and reference() takes and returns one part's arrays. A program takes and returns all parts, laid end to end along the dimension named above; an argument that names none is the same for every part. Nothing has to cross between parts.
All inputs are finite; a program needn't handle non-finite values.
Results may differ from the reference program's by a relative error of at most 0.0043.
Values may be sent and summed in bfloat16 or wider, within the bound.
A program may use at most 128 MiB of HBM per device.

```python
import math
import jax
import jax.numpy as jnp
from jax import lax

D = 768
HEADS = 12
FF = 3072
FREQ = 256
CHAN = 128
LAYERS = 1
SWEEPS = 2
GY = 8
GZ = 8
TOKENS = 1024
N_WIN = 8


def draw_w_qkv(key, part):
    base_key = jax.random.fold_in(jax.random.fold_in(key, 7), 0)
    weights = jax.random.normal(base_key, (LAYERS, D, 3 * D), jnp.float32) / jnp.sqrt(jnp.float32(D))
    return jnp.clip(weights, -2.0, 2.0).astype(jnp.bfloat16)


def set_ends(result, key, least, top_value):
    longest = result.shape.index(max(result.shape))
    spots = []
    for shift in (0, 1):
        where = [jax.random.randint(jax.random.fold_in(key, axis), (), 0, length) for axis, length in enumerate(result.shape)]
        where[longest] = (where[longest] + shift) % result.shape[longest]
        spots.append(tuple(where))
    return result.at[spots[0]].set(least).at[spots[1]].set(top_value)


def steps_of(rng, dims, shards, low, largest):
    loudness = 1.0
    for position, parts in shards:
        draws = jax.random.uniform(jax.random.fold_in(jax.random.fold_in(rng, 6), position), (parts,), jnp.float32, low / len(shards), largest / len(shards))
        loudness = loudness * jnp.repeat(jnp.exp(draws), dims[position] // parts).reshape((-1,) + (1,) * (len(dims) - 1 - position))
    return loudness


def bell_draw(key, extent, scale, most, cuts=(), kind=jnp.bfloat16):
    entries = scale * jax.random.normal(key, extent, jnp.float32)
    if cuts:
        entries = entries * steps_of(key, extent, cuts, -0.22, 0.18)
    return jnp.clip(entries, -most, most).astype(kind)


def setup_inputs(seed: int = 0, part: int = 0) -> dict:
    streams_of = jax.random.split(jax.random.key(seed), 13)
    own_keys = jax.random.split(jax.random.fold_in(streams_of[12], part), 13)
    prev_states = bell_draw(own_keys[0], (N_WIN, TOKENS, CHAN), 1.0, 6.0, ((0, 8), (1, 2)), jnp.float32)
    timesteps = set_ends(jax.random.randint(own_keys[1], (N_WIN,), 0, 1000), jax.random.fold_in(own_keys[1], 1), 0, 999).astype(jnp.int32)
    step_sizes = jnp.clip(jnp.exp(math.log(0.3) - 1.0986123 * jax.random.uniform(own_keys[2], (N_WIN,), jnp.float32) ** steps_of(own_keys[2], (N_WIN,), ((0, 8),), -0.2, 0.2)), 0.1, 0.3)
    slide = jax.random.randint(streams_of[3], (1,), 1, N_WIN + 1).astype(jnp.int32)
    w_time = bell_draw(streams_of[4], (FREQ, D), FREQ ** -0.5, 0.375)
    w_ada = bell_draw(streams_of[5], (LAYERS, D, 6 * D), D ** -0.5, 0.21875)
    w_in = bell_draw(streams_of[6], (CHAN, D), CHAN ** -0.5, 0.5)
    w_qkv = draw_w_qkv(jax.random.fold_in(streams_of[12], 71), part)
    w_proj = bell_draw(streams_of[8], (LAYERS, D, D), D ** -0.5, 0.21875)
    w_up = bell_draw(streams_of[9], (LAYERS, D, FF), D ** -0.5, 0.21875)
    w_down = bell_draw(streams_of[10], (LAYERS, FF, D), FF ** -0.5, 0.109375)
    w_out = bell_draw(streams_of[11], (D, CHAN), D ** -0.5, 0.21875)
    return {"prev_states": prev_states, "timesteps": timesteps, "step_sizes": step_sizes, "slide": slide, "w_time": w_time, "w_ada": w_ada, "w_in": w_in, "w_qkv": w_qkv, "w_proj": w_proj, "w_up": w_up, "w_down": w_down, "w_out": w_out}


EPSILON = 1e-06

def layer_norm(values):
    centred = values - lax.optimization_barrier(jnp.mean(values, axis=-1, keepdims=True))
    spread = lax.optimization_barrier(jnp.mean(centred * centred, axis=-1, keepdims=True))
    return centred * lax.rsqrt(spread + EPSILON)

def modulation(moment, w_time, w_ada):
    half = w_time.shape[0] // 2
    freqs = jnp.exp(-math.log(10000.0) * jnp.arange(half, dtype=jnp.float32) / half)
    angles = moment.astype(jnp.float32) * freqs
    embedded = jnp.concatenate([jnp.cos(angles), jnp.sin(angles)])[None, :]
    condition = jax.nn.silu(jnp.dot(embedded.astype(jnp.bfloat16), w_time, preferred_element_type=jnp.float32))
    active = jax.nn.silu(condition).astype(jnp.bfloat16)
    return jnp.stack([jnp.dot(active, w_ada[layer_index], preferred_element_type=jnp.float32).reshape(6, -1) for layer_index in range(w_ada.shape[0])])

def neighbour_mask():
    cells = jnp.arange(GY * GZ, dtype=jnp.int32)
    row_y = cells // GZ
    row_z = cells % GZ
    apart_y = (row_y[None, :] - row_y[:, None]) % GY
    apart_z = (row_z[None, :] - row_z[:, None]) % GZ
    near = (jnp.minimum(apart_y, GY - apart_y) <= 3) & (jnp.minimum(apart_z, GZ - apart_z) <= 3)
    return jnp.tile(near, (1, 7))

def attend(queries, keys, values, mask):
    planes, cells, width = queries.shape
    head_size = width // HEADS
    key_window = jnp.concatenate([keys[offset_plane:offset_plane + planes] for offset_plane in range(7)], axis=1)
    value_window = jnp.concatenate([values[offset_plane:offset_plane + planes] for offset_plane in range(7)], axis=1)
    query_heads = queries.reshape(planes, cells, HEADS, head_size).astype(jnp.float32)
    key_heads = key_window.reshape(planes, 7 * cells, HEADS, head_size).astype(jnp.float32)
    value_heads = value_window.reshape(planes, 7 * cells, HEADS, head_size).astype(jnp.float32)
    scores = jnp.einsum('pshe,pkhe->phsk', query_heads, key_heads) * head_size ** (-0.5)
    scores = jnp.where(mask, scores, -1e+30)
    peak = lax.optimization_barrier(jnp.max(scores, axis=-1, keepdims=True))
    raised = jnp.exp(scores - peak)
    weights = (raised / lax.optimization_barrier(jnp.sum(raised, axis=-1, keepdims=True))).astype(jnp.bfloat16)
    mixed = jnp.einsum('phsk,pkhe->pshe', weights.astype(jnp.float32), value_heads)
    return mixed.astype(jnp.bfloat16).reshape(planes, cells, width)

def block_layer(hidden, mods, w_qkv, w_proj, w_up, w_down, mask):
    planes, cells, width = hidden.shape
    normed = (layer_norm(hidden) * (1.0 + mods[1]) + mods[0]).astype(jnp.bfloat16)
    packed = jnp.dot(normed.reshape(-1, width), w_qkv, preferred_element_type=jnp.float32).astype(jnp.bfloat16)
    packed = packed.reshape(planes, cells, 3 * width)
    queries = packed[..., :width]
    keys = packed[..., width:2 * width]
    values = packed[..., 2 * width:]
    keys = jnp.concatenate([keys[-3:], keys, keys[:3]], axis=0)
    values = jnp.concatenate([values[-3:], values, values[:3]], axis=0)
    attended = attend(queries, keys, values, mask)
    hidden = hidden + mods[2] * jnp.dot(attended.reshape(-1, width), w_proj, preferred_element_type=jnp.float32).reshape(planes, cells, width)
    normed = (layer_norm(hidden) * (1.0 + mods[4]) + mods[3]).astype(jnp.bfloat16)
    inner = jax.nn.gelu(jnp.dot(normed.reshape(-1, width), w_up, preferred_element_type=jnp.float32), approximate=True).astype(jnp.bfloat16)
    return hidden + mods[5] * jnp.dot(inner, w_down, preferred_element_type=jnp.float32).reshape(planes, cells, width)

def field_drift(states_now, mod_rows, weights, mask):
    w_in, w_qkv, w_proj, w_up, w_down, w_out = weights
    cells = GY * GZ
    planes = states_now.shape[0] // cells
    hidden = jnp.dot(states_now.astype(jnp.bfloat16), w_in, preferred_element_type=jnp.float32).reshape(planes, cells, -1)
    for layer_index in range(w_qkv.shape[0]):
        hidden = block_layer(hidden, mod_rows[layer_index], w_qkv[layer_index], w_proj[layer_index], w_up[layer_index], w_down[layer_index], mask)
    width = hidden.shape[-1]
    return jnp.dot(layer_norm(hidden).astype(jnp.bfloat16).reshape(-1, width), w_out, preferred_element_type=jnp.float32)

def reference(prev_states, timesteps, step_sizes, slide, w_time, w_ada, w_in, w_qkv, w_proj, w_up, w_down, w_out):
    window = N_WIN
    offset = (slide[0] - 1).astype(jnp.int32)
    targets = jnp.minimum(jnp.arange(window, dtype=jnp.int32) + offset, window - 1).astype(jnp.int32)
    iterate = jnp.take(prev_states, targets, axis=0)
    start = lax.dynamic_index_in_dim(prev_states, offset, 0, keepdims=False)
    mask = neighbour_mask()
    weights = (w_in, w_qkv, w_proj, w_up, w_down, w_out)

    def one_drift(pair):
        states_now, moment = pair
        return field_drift(states_now, modulation(moment, w_time, w_ada), weights, mask)
    total = iterate
    for sweep_index in range(SWEEPS):
        drift = lax.map(one_drift, (iterate, timesteps))
        increment = step_sizes[:, None, None] * drift
        total = jnp.cumsum(increment, axis=0)
        iterate = start[None] + (total - increment)
    return start[None] + total
```

```python
import functools
import math

import jax
import jax.numpy as jnp
import numpy as np
from jax import lax
from jax.experimental import pallas as pl
from jax.experimental.pallas import tpu as pltpu
from jax.sharding import PartitionSpec as P

HEADS = 12
SWEEPS = 2
GY = 8
GZ = 8
REACH = 3
EPSILON = 1e-06
MESH = pl.DeviceIdType.MESH
F32 = jnp.float32
BF16 = jnp.bfloat16


def modulation(moment, w_time, w_ada):
    half = w_time.shape[0] // 2
    freqs = jnp.exp(-math.log(10000.0) * jnp.arange(half, dtype=F32) / half)
    angles = moment.astype(F32) * freqs
    embedded = jnp.concatenate([jnp.cos(angles), jnp.sin(angles)])[None, :]
    condition = jax.nn.silu(jnp.dot(embedded.astype(BF16), w_time, preferred_element_type=F32))
    active = jax.nn.silu(condition).astype(BF16)
    return jnp.dot(active, w_ada[0], preferred_element_type=F32).reshape(6, -1)


def pair_bias():
    cells = GY * GZ
    query = np.arange(2 * cells)[:, None]
    key = np.arange((2 * REACH + 2) * cells)[None, :]
    apart_x = key // cells - query // cells
    apart_y = (key % cells // GZ - query % cells // GZ) % GY
    apart_z = (key % GZ - query % GZ) % GZ
    near = (apart_x >= 0) & (apart_x <= 2 * REACH)
    near &= (np.minimum(apart_y, GY - apart_y) <= REACH) & (np.minimum(apart_z, GZ - apart_z) <= REACH)
    bias = np.where(near, 0.0, -1e30).astype(np.float32)
    return np.concatenate([bias, bias], axis=0)


def greet(peers):
    barrier = pltpu.get_barrier_semaphore()
    for peer in peers:
        pl.semaphore_signal(barrier, inc=1, device_id=peer, device_id_type=MESH)
    pl.semaphore_wait(barrier, len(peers))


def swap_rims(ext, send_sem, recv_sem, gx):
    side = lax.axis_index("gx")
    rim = REACH * GY * GZ
    rows = ext.shape[0]
    copies = [
        pltpu.make_async_remote_copy(
            src_ref=ext.at[pl.ds(rows - 2 * rim, rim)],
            dst_ref=ext.at[pl.ds(0, rim)],
            send_sem=send_sem.at[0],
            recv_sem=recv_sem.at[0],
            device_id={"gx": lax.rem(side + 1, gx)},
            device_id_type=MESH,
        ),
        pltpu.make_async_remote_copy(
            src_ref=ext.at[pl.ds(rim, rim)],
            dst_ref=ext.at[pl.ds(rows - rim, rim)],
            send_sem=send_sem.at[1],
            recv_sem=recv_sem.at[1],
            device_id={"gx": lax.rem(side + gx - 1, gx)},
            device_id_type=MESH,
        ),
    ]
    for copy in copies:
        copy.start()
    for copy in copies:
        copy.wait()


def shift_kernel(
    offset, window, gx, prev, ext, fine, own, own_fine, send_sem, recv_sem, fine_send, fine_recv, rim_send, rim_recv
):
    me, side = lax.axis_index("win"), lax.axis_index("gx")
    rows = prev.shape[0]
    rim = REACH * GY * GZ
    own[...] = prev[...].astype(BF16)
    own_fine[...] = (prev[...] - own[...].astype(F32)).astype(BF16)
    peers = [{"gx": lax.rem(side + 1, gx)}]
    peers += [{"win": lax.rem(me + d, window)} for d in range(1, window)] if offset else []
    greet(peers)

    def copy_to(target, slot):
        return pltpu.make_async_remote_copy(
            src_ref=own,
            dst_ref=ext.at[pl.ds(rim, rows)],
            send_sem=send_sem.at[slot],
            recv_sem=recv_sem,
            device_id={"win": target},
            device_id_type=MESH,
        )

    last = window - 1
    fine_copy = pltpu.make_async_remote_copy(
        src_ref=own_fine,
        dst_ref=fine,
        send_sem=fine_send,
        recv_sem=fine_recv,
        device_id={"win": 0},
        device_id_type=MESH,
    )

    @pl.when(me > 0)
    def _():
        fine[...] = jnp.zeros_like(fine)

    if offset:

        @pl.when(me == last)
        def _():
            for t in range(last - offset, last):
                copy_to(t, t).start()

        if offset < last:

            @pl.when((me < last) & (me >= offset))
            def _():
                copy_to(me - offset, last).start()

        @pl.when(me == offset)
        def _():
            fine_copy.start()

        @pl.when(me == last)
        def _():
            ext[pl.ds(rim, rows), :] = own[...]

        @pl.when(me < last)
        def _():
            copy_to(me, 0).wait_recv()

    else:
        ext[pl.ds(rim, rows), :] = own[...]

        @pl.when(me == 0)
        def _():
            fine[...] = own_fine[...]

    swap_rims(ext, rim_send, rim_recv, gx)
    if offset:

        @pl.when(me == last)
        def _():
            for t in range(last - offset, last):
                copy_to(t, t).wait_send()

        if offset < last:

            @pl.when((me < last) & (me >= offset))
            def _():
                copy_to(me - offset, last).wait_send()

        @pl.when(me == offset)
        def _():
            fine_copy.wait_send()

        @pl.when(me == 0)
        def _():
            fine_copy.wait_recv()


def shifted(prev, offset, window, gx):
    rows, channels = prev.shape
    ext_rows = rows + 2 * REACH * GY * GZ

    def branch(static):
        def call(x):
            return pl.pallas_call(
                functools.partial(shift_kernel, static, window, gx),
                out_shape=[
                    jax.ShapeDtypeStruct((ext_rows, channels), BF16),
                    jax.ShapeDtypeStruct((rows, channels), BF16),
                ],
                in_specs=[pl.BlockSpec(memory_space=pltpu.VMEM)],
                out_specs=[pl.BlockSpec(memory_space=pltpu.VMEM)] * 2,
                scratch_shapes=[
                    pltpu.VMEM((rows, channels), BF16),
                    pltpu.VMEM((rows, channels), BF16),
                    pltpu.SemaphoreType.DMA((window,)),
                    pltpu.SemaphoreType.DMA,
                    pltpu.SemaphoreType.DMA,
                    pltpu.SemaphoreType.DMA,
                    pltpu.SemaphoreType.DMA((2,)),
                    pltpu.SemaphoreType.DMA((2,)),
                ],
                compiler_params=pltpu.CompilerParams(collective_id=2 + static, has_side_effects=True),
                name=f"shift_{static}",
            )(x)

        return call

    return lax.switch(offset, [branch(static) for static in range(window)], prev)


def scan_kernel(
    final, window, gx, inc, ext_in, fine, out,
    contrib, partner, half_sum, slots, fine_sum, fine_slot, half_before, back_from, back_into, before,
    pair_send, pair_recv, far_send, far_recv, fine_send, fine_recv, back_send, back_recv, rim_send, rim_recv,
):
    me, side = lax.axis_index("win"), lax.axis_index("gx")
    rows = inc.shape[0]
    half = rows // 2
    rim = REACH * GY * GZ
    groups = window // 2
    z, y = me // 2, lax.rem(me, 2)
    mate = {"win": me + 1 - 2 * y}

    opening = jnp.where(me == 0, ext_in[pl.ds(rim, rows), :].astype(F32) + fine[...].astype(F32), 0.0)
    contrib[...] = (inc[...] + opening).astype(contrib.dtype)
    peers = [mate]
    peers += [{"win": lax.rem(me + 2 * d, window)} for d in range(1, groups)]
    if not final:
        peers.append({"gx": lax.rem(side + 1, gx)})
    greet(peers)

    def pair_copy(part):
        return pltpu.make_async_remote_copy(
            src_ref=contrib.at[pl.ds(part * half, half)],
            dst_ref=partner.at[pl.ds(part * half, half)],
            send_sem=pair_send.at[part],
            recv_sem=pair_recv.at[part],
            device_id=mate,
            device_id_type=MESH,
        )

    def far_copy(target, slot):
        return pltpu.make_async_remote_copy(
            src_ref=half_sum,
            dst_ref=slots.at[slot],
            send_sem=far_send.at[target],
            recv_sem=far_recv.at[slot],
            device_id={"win": target * 2 + y},
            device_id_type=MESH,
        )

    def fine_copy(target):
        return pltpu.make_async_remote_copy(
            src_ref=fine_sum,
            dst_ref=fine_slot,
            send_sem=fine_send.at[target],
            recv_sem=fine_recv,
            device_id={"win": target * 2 + y},
            device_id_type=MESH,
        )

    back_copy = pltpu.make_async_remote_copy(
        src_ref=back_from,
        dst_ref=back_into,
        send_sem=back_send,
        recv_sem=back_recv,
        device_id=mate,
        device_id_type=MESH,
    )

    @pl.when(y == 0)
    def _():
        pair_copy(1).start()
        pair_copy(0).start()
        pair_copy(0).wait_recv()
        share = contrib[:half, :].astype(F32) + partner[:half, :].astype(F32)
        half_sum[...] = share.astype(BF16)
        fine_sum[...] = (share - share.astype(BF16).astype(F32)).astype(BF16)

    @pl.when(y == 1)
    def _():
        pair_copy(0).start()
        pair_copy(1).wait_recv()
        share = contrib[half:, :].astype(F32) + partner[half:, :].astype(F32)
        half_sum[...] = share.astype(BF16)
        fine_sum[...] = (share - share.astype(BF16).astype(F32)).astype(BF16)

    for target in range(1, groups):
        for source in range(target):

            @pl.when(z == source)
            def _():
                far_copy(target, source).start()
                if final and source == 0:
                    fine_copy(target).start()

    half_before[...] = jnp.zeros_like(half_before)
    for source in range(groups - 1):

        @pl.when(z > source)
        def _():
            far_copy(source + 1, source).wait_recv()
            half_before[...] += slots[source].astype(F32)
            if final and source == 0:
                fine_copy(1).wait_recv()
                half_before[...] += fine_slot[...].astype(F32)

    before[...] = jnp.zeros_like(before)

    @pl.when(z > 0)
    def _():
        back_from[...] = half_before[...].astype(back_from.dtype)
        back_copy.start()
        back_copy.wait_recv()

    @pl.when((z > 0) & (y == 0))
    def _():
        before[:half, :] = half_before[...]
        before[half:, :] = back_into[...].astype(F32)

    @pl.when((z > 0) & (y == 1))
    def _():
        before[:half, :] = back_into[...].astype(F32)
        before[half:, :] = half_before[...]

    @pl.when(y == 1)
    def _():
        pair_copy(0).wait_recv()
        before[...] += partner[...].astype(F32)

    if final:
        out[...] = before[...] + (inc[...] + opening)
    else:
        out[pl.ds(rim, rows), :] = jnp.where(me == 0, opening, before[...]).astype(BF16)
        swap_rims(out, rim_send, rim_recv, gx)

    pair_copy(0).wait_send()

    @pl.when(y == 0)
    def _():
        pair_copy(1).wait_send()

    for target in range(1, groups):

        @pl.when(z < target)
        def _():
            far_copy(target, 0).wait_send()

        if final:

            @pl.when(z == 0)
            def _():
                fine_copy(target).wait_send()

    @pl.when(z > 0)
    def _():
        back_copy.wait_send()


def scanned(inc, ext, fine, window, gx, final):
    kind = F32 if final else BF16
    rows, channels = inc.shape
    half, groups = rows // 2, window // 2
    return pl.pallas_call(
        functools.partial(scan_kernel, final, window, gx),
        out_shape=jax.ShapeDtypeStruct(inc.shape, F32) if final else jax.ShapeDtypeStruct(ext.shape, BF16),
        in_specs=[pl.BlockSpec(memory_space=pltpu.VMEM)] * 3,
        out_specs=pl.BlockSpec(memory_space=pltpu.VMEM),
        scratch_shapes=[
            pltpu.VMEM((rows, channels), kind),
            pltpu.VMEM((rows, channels), kind),
            pltpu.VMEM((half, channels), BF16),
            pltpu.VMEM((groups, half, channels), BF16),
            pltpu.VMEM((half, channels), BF16),
            pltpu.VMEM((half, channels), BF16),
            pltpu.VMEM((half, channels), F32),
            pltpu.VMEM((half, channels), kind),
            pltpu.VMEM((half, channels), kind),
            pltpu.VMEM((rows, channels), F32),
            pltpu.SemaphoreType.DMA((2,)),
            pltpu.SemaphoreType.DMA((2,)),
            pltpu.SemaphoreType.DMA((groups,)),
            pltpu.SemaphoreType.DMA((groups,)),
            pltpu.SemaphoreType.DMA((groups,)),
            pltpu.SemaphoreType.DMA,
            pltpu.SemaphoreType.DMA,
            pltpu.SemaphoreType.DMA,
            pltpu.SemaphoreType.DMA((2,)),
            pltpu.SemaphoreType.DMA((2,)),
        ],
        compiler_params=pltpu.CompilerParams(collective_id=int(final), has_side_effects=True),
        name="scan_final" if final else "scan_next",
    )(inc, ext, fine)


def normalised(values):
    centred = values - jnp.mean(values, axis=-1, keepdims=True)
    spread = jnp.mean(centred * centred, axis=-1, keepdims=True)
    return centred * lax.rsqrt(spread + EPSILON)


def drift_kernel(
    ext, mods, step, bias, w_in_hbm, w_qkv_hbm, w_proj_hbm, w_up_hbm, w_down_hbm, w_out_hbm, inc,
    w_in, w_qkv, w_proj, w_up, w_down, w_out, hidden, normed, queries, keys, values, mixed, ff, sems,
):
    cells = GY * GZ
    rim = REACH * cells
    ext_rows = ext.shape[0]
    rows = inc.shape[0]
    width = hidden.shape[1]
    pair = 2 * width // HEADS
    pairs = HEADS // 2
    loads = [
        pltpu.make_async_copy(source, target, sems.at[i])
        for i, (source, target) in enumerate(
            [
                (w_in_hbm, w_in),
                (w_qkv_hbm, w_qkv),
                (w_proj_hbm, w_proj),
                (w_up_hbm, w_up),
                (w_down_hbm, w_down),
                (w_out_hbm, w_out),
            ]
        )
    ]
    for load in loads:
        load.start()
    shift1, scale1, gate1 = mods[0:1, :], mods[1:2, :], mods[2:3, :]
    shift2, scale2, gate2 = mods[3:4, :], mods[4:5, :], mods[5:6, :]

    loads[0].wait()
    chunk = 2 * cells

    @pl.loop(0, ext_rows // chunk)
    def _(i):
        at = pl.ds(pl.multiple_of(i * chunk, chunk), chunk)
        h = jnp.dot(ext[at, :], w_in[...], preferred_element_type=F32)
        hidden[at, :] = h
        normed[at, :] = (normalised(h) * (1.0 + scale1) + shift1).astype(BF16)
        values[at, :] = jnp.ones((chunk, 2 * width), BF16)

    loads[1].wait()
    inner = pl.ds(rim, rows)
    for j in range(pairs):
        part = slice(j * pair, (j + 1) * pair)
        queries[:, part] = (
            jnp.dot(normed[inner, :], w_qkv[:, part], preferred_element_type=F32) * (pair // 2) ** -0.5
        ).astype(BF16)
        keys[:, part] = jnp.dot(
            normed[...], w_qkv[:, width + j * pair : width + (j + 1) * pair], preferred_element_type=F32
        ).astype(BF16)
        values[:, 2 * j * pair : (2 * j + 1) * pair] = jnp.dot(
            normed[...], w_qkv[:, 2 * width + j * pair : 2 * width + (j + 1) * pair], preferred_element_type=F32
        ).astype(BF16)

    first = lax.broadcasted_iota(jnp.int32, (chunk, pair), 1) < pair // 2
    span = chunk + 2 * rim

    @pl.loop(0, rows // chunk)
    def _(i):
        at = pl.ds(pl.multiple_of(i * chunk, chunk), chunk)
        window = pl.ds(pl.multiple_of(i * chunk, chunk), span)
        for j in range(pairs):
            part = slice(j * pair, (j + 1) * pair)
            q = queries[at, part]
            zero = jnp.zeros_like(q)
            stacked = jnp.concatenate([jnp.where(first, q, zero), jnp.where(first, zero, q)], axis=0)
            scores = lax.dot_general(
                stacked, keys[window, part], (((1,), (1,)), ((), ())), preferred_element_type=F32
            )
            scores = scores + bias[...]
            peak = jnp.max(scores, axis=-1, keepdims=True)
            raised = jnp.exp(scores - peak).astype(BF16)
            both = jnp.dot(raised, values[window, 2 * j * pair : 2 * (j + 1) * pair], preferred_element_type=F32)
            ratio = both[:, :pair] / both[:, pair:]
            mixed[at, part] = jnp.where(first, ratio[:chunk], ratio[chunk:]).astype(BF16)

    loads[2].wait()
    block = rows // 2

    @pl.loop(0, rows // block)
    def _(i):
        at = pl.ds(pl.multiple_of(i * block, block), block)
        centre = pl.ds(pl.multiple_of(rim + i * block, cells), block)
        h = hidden[centre, :] + gate1 * jnp.dot(mixed[at, :], w_proj[...], preferred_element_type=F32)
        hidden[centre, :] = h
        normed[at, :] = (normalised(h) * (1.0 + scale2) + shift2).astype(BF16)

    loads[3].wait()
    loads[4].wait()
    ff[...] = jnp.zeros_like(ff)
    slab = width

    @pl.loop(0, w_up.shape[1] // slab)
    def _(c):
        at = pl.ds(pl.multiple_of(c * slab, slab), slab)
        up = jnp.dot(normed[:rows, :], w_up[:, at], preferred_element_type=F32)
        up = jax.nn.gelu(up, approximate=True).astype(BF16)
        ff[...] += jnp.dot(up, w_down[at, :], preferred_element_type=F32)

    loads[5].wait()
    h = hidden[inner, :] + gate2 * ff[...]
    inc[...] = step[...] * jnp.dot(normalised(h).astype(BF16), w_out[...], preferred_element_type=F32)


def scaled_drift(ext, mods, step, bias, weights):
    rim = REACH * GY * GZ
    ext_rows, channels = ext.shape
    rows = ext_rows - 2 * rim
    width = weights[0].shape[1]
    vmem = pl.BlockSpec(memory_space=pltpu.VMEM)
    scratch = [pltpu.VMEM(w.shape, w.dtype) for w in weights] + [
        pltpu.VMEM((ext_rows, width), F32),
        pltpu.VMEM((ext_rows, width), BF16),
        pltpu.VMEM((rows, width), BF16),
        pltpu.VMEM((ext_rows, width), BF16),
        pltpu.VMEM((ext_rows, 2 * width), BF16),
        pltpu.VMEM((rows, width), BF16),
        pltpu.VMEM((rows, width), F32),
        pltpu.SemaphoreType.DMA((len(weights),)),
    ]
    return pl.pallas_call(
        drift_kernel,
        out_shape=jax.ShapeDtypeStruct((rows, channels), F32),
        in_specs=[vmem] * 4 + [pl.BlockSpec(memory_space=pl.ANY)] * len(weights),
        out_specs=vmem,
        scratch_shapes=scratch,
        compiler_params=pltpu.CompilerParams(vmem_limit_bytes=56 * 1024 * 1024),
        name="drift",
    )(ext, mods, step, bias, *weights)


def local(prev_states, timesteps, step_sizes, slide, w_time, w_ada, w_in, w_qkv, w_proj, w_up, w_down, w_out):
    window, gx = lax.axis_size("win"), lax.axis_size("gx")
    mods = modulation(timesteps[0], w_time, w_ada)
    weights = (w_in, w_qkv[0], w_proj[0], w_up[0], w_down[0], w_out)
    step = jnp.broadcast_to(step_sizes[None, :], (1, prev_states.shape[2]))
    bias = jnp.asarray(pair_bias())
    opening, fine = shifted(prev_states[0], slide[0] - 1, window, gx)
    ext = opening
    for sweep in range(SWEEPS):
        inc = scaled_drift(ext, mods, step, bias, weights)
        ext = scanned(inc, opening, fine, window, gx, sweep == SWEEPS - 1)
    return ext[None]


def solution(mesh):
    spread, split, whole = P(("groups", "win"), "gx", None), P(("groups", "win")), P()
    return jax.shard_map(
        local,
        mesh=mesh,
        in_specs=(spread, split, split) + (whole,) * 9,
        out_specs=spread,
        check_vma=False,
    )
```

```python
import functools
import math

import jax
import jax.numpy as jnp
import numpy as np
from jax import lax
from jax.experimental import pallas as pl
from jax.experimental.pallas import tpu as pltpu
from jax.sharding import PartitionSpec as P

HEADS = 12
SWEEPS = 2
GY = 8
GZ = 8
REACH = 3
EPSILON = 1e-06
MESH = pl.DeviceIdType.MESH
F32 = jnp.float32
BF16 = jnp.bfloat16


def project_kernel(active, w_ada, mods):
    mods[...] = jnp.dot(active[...], w_ada[...], preferred_element_type=F32)


def modulation(moment, w_time, w_ada):
    half = w_time.shape[0] // 2
    freqs = jnp.exp(-math.log(10000.0) * jnp.arange(half, dtype=F32) / half)
    angles = moment.astype(F32) * freqs
    embedded = jnp.concatenate([jnp.cos(angles), jnp.sin(angles)])[None, :]
    condition = jax.nn.silu(jnp.dot(embedded.astype(BF16), w_time, preferred_element_type=F32))
    active = jnp.broadcast_to(jax.nn.silu(condition).astype(BF16), (16, w_time.shape[1]))
    width, columns = w_ada.shape[1:]
    return pl.pallas_call(
        project_kernel,
        out_shape=jax.ShapeDtypeStruct((16, columns), F32),
        grid=(columns // width,),
        in_specs=[
            pl.BlockSpec((16, width), lambda i: (0, 0)),
            pl.BlockSpec((width, width), lambda i: (0, i)),
        ],
        out_specs=pl.BlockSpec((16, width), lambda i: (0, i)),
        compiler_params=pltpu.CompilerParams(vmem_limit_bytes=56 * 1024 * 1024),
        name="modulate",
    )(active, w_ada[0])


def pair_bias():
    cells = GY * GZ
    query = np.arange(2 * cells)[:, None]
    key = np.arange((2 * REACH + 2) * cells)[None, :]
    apart_x = key // cells - query // cells
    apart_y = (key % cells // GZ - query % cells // GZ) % GY
    apart_z = (key % GZ - query % GZ) % GZ
    near = (apart_x >= 0) & (apart_x <= 2 * REACH)
    near &= (np.minimum(apart_y, GY - apart_y) <= REACH) & (np.minimum(apart_z, GZ - apart_z) <= REACH)
    bias = np.where(near, 0.0, -1e30).astype(np.float32)
    return np.concatenate([bias, bias], axis=0)


def greet(peers):
    barrier = pltpu.get_barrier_semaphore()
    for peer in peers:
        pl.semaphore_signal(barrier, inc=1, device_id=peer, device_id_type=MESH)
    pl.semaphore_wait(barrier, len(peers))


def swap_rims(ext, send_sem, recv_sem, gx):
    side = lax.axis_index("gx")
    rim = REACH * GY * GZ
    rows = ext.shape[0]
    copies = [
        pltpu.make_async_remote_copy(
            src_ref=ext.at[pl.ds(rows - 2 * rim, rim)],
            dst_ref=ext.at[pl.ds(0, rim)],
            send_sem=send_sem.at[0],
            recv_sem=recv_sem.at[0],
            device_id={"gx": lax.rem(side + 1, gx)},
            device_id_type=MESH,
        ),
        pltpu.make_async_remote_copy(
            src_ref=ext.at[pl.ds(rim, rim)],
            dst_ref=ext.at[pl.ds(rows - rim, rim)],
            send_sem=send_sem.at[1],
            recv_sem=recv_sem.at[1],
            device_id={"gx": lax.rem(side + gx - 1, gx)},
            device_id_type=MESH,
        ),
    ]
    for copy in copies:
        copy.start()
    for copy in copies:
        copy.wait()


def shift_kernel(
    offset, window, gx, prev, ext, fine, own, own_fine, send_sem, recv_sem, fine_send, fine_recv, rim_send, rim_recv
):
    me, side = lax.axis_index("win"), lax.axis_index("gx")
    rows = prev.shape[0]
    rim = REACH * GY * GZ
    own[...] = prev[...].astype(BF16)
    own_fine[...] = (prev[...] - own[...].astype(F32)).astype(BF16)
    peers = [{"gx": lax.rem(side + 1, gx)}]
    peers += [{"win": lax.rem(me + d, window)} for d in range(1, window)] if offset else []
    greet(peers)

    def copy_to(target, slot):
        return pltpu.make_async_remote_copy(
            src_ref=own,
            dst_ref=ext.at[pl.ds(rim, rows)],
            send_sem=send_sem.at[slot],
            recv_sem=recv_sem,
            device_id={"win": target},
            device_id_type=MESH,
        )

    last = window - 1
    fine_copy = pltpu.make_async_remote_copy(
        src_ref=own_fine,
        dst_ref=fine,
        send_sem=fine_send,
        recv_sem=fine_recv,
        device_id={"win": 0},
        device_id_type=MESH,
    )

    @pl.when(me > 0)
    def _():
        fine[...] = jnp.zeros_like(fine)

    if offset:

        @pl.when(me == last)
        def _():
            for t in range(last - offset, last):
                copy_to(t, t).start()

        if offset < last:

            @pl.when((me < last) & (me >= offset))
            def _():
                copy_to(me - offset, last).start()

        @pl.when(me == offset)
        def _():
            fine_copy.start()

        @pl.when(me == last)
        def _():
            ext[pl.ds(rim, rows), :] = own[...]

        @pl.when(me < last)
        def _():
            copy_to(me, 0).wait_recv()

    else:
        ext[pl.ds(rim, rows), :] = own[...]

        @pl.when(me == 0)
        def _():
            fine[...] = own_fine[...]

    swap_rims(ext, rim_send, rim_recv, gx)
    if offset:

        @pl.when(me == last)
        def _():
            for t in range(last - offset, last):
                copy_to(t, t).wait_send()

        if offset < last:

            @pl.when((me < last) & (me >= offset))
            def _():
                copy_to(me - offset, last).wait_send()

        @pl.when(me == offset)
        def _():
            fine_copy.wait_send()

        @pl.when(me == 0)
        def _():
            fine_copy.wait_recv()


def shifted(prev, offset, window, gx):
    rows, channels = prev.shape
    ext_rows = rows + 2 * REACH * GY * GZ

    def branch(static):
        def call(x):
            return pl.pallas_call(
                functools.partial(shift_kernel, static, window, gx),
                out_shape=[
                    jax.ShapeDtypeStruct((ext_rows, channels), BF16),
                    jax.ShapeDtypeStruct((rows, channels), BF16),
                ],
                in_specs=[pl.BlockSpec(memory_space=pltpu.VMEM)],
                out_specs=[pl.BlockSpec(memory_space=pltpu.VMEM)] * 2,
                scratch_shapes=[
                    pltpu.VMEM((rows, channels), BF16),
                    pltpu.VMEM((rows, channels), BF16),
                    pltpu.SemaphoreType.DMA((window,)),
                    pltpu.SemaphoreType.DMA,
                    pltpu.SemaphoreType.DMA,
                    pltpu.SemaphoreType.DMA,
                    pltpu.SemaphoreType.DMA((2,)),
                    pltpu.SemaphoreType.DMA((2,)),
                ],
                compiler_params=pltpu.CompilerParams(collective_id=2 + static, has_side_effects=True),
                name=f"shift_{static}",
            )(x)

        return call

    return lax.switch(offset, [branch(static) for static in range(window)], prev)


def scan_kernel(
    final, window, gx, inc, ext_in, out,
    contrib, partner, half_sum, slots, half_before, back_from, back_into, before,
    pair_send, pair_recv, far_send, far_recv, back_send, back_recv, rim_send, rim_recv,
):
    me, side = lax.axis_index("win"), lax.axis_index("gx")
    rows = inc.shape[0]
    half = rows // 2
    rim = REACH * GY * GZ
    groups = window // 2
    z, y = me // 2, lax.rem(me, 2)
    mate = {"win": me + 1 - 2 * y}

    if final:
        contrib[...] = inc[...].astype(BF16)
    else:
        opening = jnp.where(me == 0, ext_in[pl.ds(rim, rows), :].astype(F32), 0.0)
        contrib[...] = (inc[...] + opening).astype(BF16)
    peers = [mate]
    peers += [{"win": lax.rem(me + 2 * d, window)} for d in range(1, groups)]
    if not final:
        peers.append({"gx": lax.rem(side + 1, gx)})
    greet(peers)

    def pair_copy(part):
        return pltpu.make_async_remote_copy(
            src_ref=contrib.at[pl.ds(part * half, half)],
            dst_ref=partner.at[pl.ds(part * half, half)],
            send_sem=pair_send.at[part],
            recv_sem=pair_recv.at[part],
            device_id=mate,
            device_id_type=MESH,
        )

    def far_copy(target, slot):
        return pltpu.make_async_remote_copy(
            src_ref=half_sum,
            dst_ref=slots.at[slot],
            send_sem=far_send.at[target],
            recv_sem=far_recv.at[slot],
            device_id={"win": target * 2 + y},
            device_id_type=MESH,
        )

    back_copy = pltpu.make_async_remote_copy(
        src_ref=back_from,
        dst_ref=back_into,
        send_sem=back_send,
        recv_sem=back_recv,
        device_id=mate,
        device_id_type=MESH,
    )

    @pl.when(y == 0)
    def _():
        pair_copy(1).start()
        pair_copy(0).start()
        pair_copy(0).wait_recv()
        half_sum[...] = (contrib[:half, :].astype(F32) + partner[:half, :].astype(F32)).astype(BF16)

    @pl.when(y == 1)
    def _():
        pair_copy(0).start()
        pair_copy(1).wait_recv()
        half_sum[...] = (contrib[half:, :].astype(F32) + partner[half:, :].astype(F32)).astype(BF16)

    for target in range(1, groups):
        for source in range(target):

            @pl.when(z == source)
            def _():
                far_copy(target, source).start()

    half_before[...] = jnp.zeros_like(half_before)
    for source in range(groups - 1):

        @pl.when(z > source)
        def _():
            far_copy(source + 1, source).wait_recv()
            half_before[...] += slots[source].astype(F32)

    before[...] = jnp.zeros_like(before)

    @pl.when(z > 0)
    def _():
        back_from[...] = half_before[...].astype(BF16)
        back_copy.start()
        back_copy.wait_recv()

    @pl.when((z > 0) & (y == 0))
    def _():
        before[:half, :] = half_before[...]
        before[half:, :] = back_into[...].astype(F32)

    @pl.when((z > 0) & (y == 1))
    def _():
        before[:half, :] = back_into[...].astype(F32)
        before[half:, :] = half_before[...]

    @pl.when(y == 1)
    def _():
        pair_copy(0).wait_recv()
        before[...] += partner[...].astype(F32)

    if final:
        out[...] = before[...] + inc[...]
    else:
        out[pl.ds(rim, rows), :] = jnp.where(me == 0, opening, before[...]).astype(BF16)
        swap_rims(out, rim_send, rim_recv, gx)

    pair_copy(0).wait_send()

    @pl.when(y == 0)
    def _():
        pair_copy(1).wait_send()

    for target in range(1, groups):

        @pl.when(z < target)
        def _():
            far_copy(target, 0).wait_send()

    @pl.when(z > 0)
    def _():
        back_copy.wait_send()


def scanned(inc, ext, window, gx, final):
    rows, channels = inc.shape
    half, groups = rows // 2, window // 2
    return pl.pallas_call(
        functools.partial(scan_kernel, final, window, gx),
        out_shape=jax.ShapeDtypeStruct(inc.shape, F32) if final else jax.ShapeDtypeStruct(ext.shape, BF16),
        in_specs=[pl.BlockSpec(memory_space=pltpu.VMEM)] * 2,
        out_specs=pl.BlockSpec(memory_space=pltpu.VMEM),
        scratch_shapes=[
            pltpu.VMEM((rows, channels), BF16),
            pltpu.VMEM((rows, channels), BF16),
            pltpu.VMEM((half, channels), BF16),
            pltpu.VMEM((groups, half, channels), BF16),
            pltpu.VMEM((half, channels), F32),
            pltpu.VMEM((half, channels), BF16),
            pltpu.VMEM((half, channels), BF16),
            pltpu.VMEM((rows, channels), F32),
            pltpu.SemaphoreType.DMA((2,)),
            pltpu.SemaphoreType.DMA((2,)),
            pltpu.SemaphoreType.DMA((groups,)),
            pltpu.SemaphoreType.DMA((groups,)),
            pltpu.SemaphoreType.DMA,
            pltpu.SemaphoreType.DMA,
            pltpu.SemaphoreType.DMA((2,)),
            pltpu.SemaphoreType.DMA((2,)),
        ],
        compiler_params=pltpu.CompilerParams(collective_id=int(final), has_side_effects=True),
        name="scan_final" if final else "scan_next",
    )(inc, ext)


def normalised(values):
    centred = values - jnp.mean(values, axis=-1, keepdims=True)
    spread = jnp.mean(centred * centred, axis=-1, keepdims=True)
    return centred * lax.rsqrt(spread + EPSILON)


def drift_kernel(
    ext, mods, step, bias, w_in_hbm, w_qkv_hbm, w_proj_hbm, w_up_hbm, w_down_hbm, w_out_hbm, inc,
    w_in, w_qkv, w_proj, w_up, w_down, w_out, hidden, normed, queries, keys, values, mixed, ff, sems,
):
    cells = GY * GZ
    rim = REACH * cells
    ext_rows = ext.shape[0]
    rows = inc.shape[0]
    width = hidden.shape[1]
    pair = 2 * width // HEADS
    pairs = HEADS // 2
    loads = [
        pltpu.make_async_copy(source, target, sems.at[i])
        for i, (source, target) in enumerate(
            [
                (w_in_hbm, w_in),
                (w_qkv_hbm, w_qkv),
                (w_proj_hbm, w_proj),
                (w_up_hbm, w_up),
                (w_down_hbm, w_down),
                (w_out_hbm, w_out),
            ]
        )
    ]
    for load in loads:
        load.start()
    shift1, scale1, gate1, shift2, scale2, gate2 = [mods[0:1, i * width : (i + 1) * width] for i in range(6)]

    loads[0].wait()
    chunk = 2 * cells

    @pl.loop(0, ext_rows // chunk)
    def _(i):
        at = pl.ds(pl.multiple_of(i * chunk, chunk), chunk)
        h = jnp.dot(ext[at, :], w_in[...], preferred_element_type=F32)
        hidden[at, :] = h
        normed[at, :] = (normalised(h) * (1.0 + scale1) + shift1).astype(BF16)
        values[at, :] = jnp.ones((chunk, 2 * width), BF16)

    loads[1].wait()
    inner = pl.ds(rim, rows)
    for j in range(pairs):
        part = slice(j * pair, (j + 1) * pair)
        queries[:, part] = (
            jnp.dot(normed[inner, :], w_qkv[:, part], preferred_element_type=F32) * (pair // 2) ** -0.5
        ).astype(BF16)
        keys[:, part] = jnp.dot(
            normed[...], w_qkv[:, width + j * pair : width + (j + 1) * pair], preferred_element_type=F32
        ).astype(BF16)
        values[:, 2 * j * pair : (2 * j + 1) * pair] = jnp.dot(
            normed[...], w_qkv[:, 2 * width + j * pair : 2 * width + (j + 1) * pair], preferred_element_type=F32
        ).astype(BF16)

    first = lax.broadcasted_iota(jnp.int32, (chunk, pair), 1) < pair // 2
    span = chunk + 2 * rim

    @pl.loop(0, rows // chunk)
    def _(i):
        at = pl.ds(pl.multiple_of(i * chunk, chunk), chunk)
        window = pl.ds(pl.multiple_of(i * chunk, chunk), span)
        for j in range(pairs):
            part = slice(j * pair, (j + 1) * pair)
            q = queries[at, part]
            zero = jnp.zeros_like(q)
            stacked = jnp.concatenate([jnp.where(first, q, zero), jnp.where(first, zero, q)], axis=0)
            scores = lax.dot_general(
                stacked, keys[window, part], (((1,), (1,)), ((), ())), preferred_element_type=F32
            )
            scores = scores + bias[...]
            peak = jnp.max(scores, axis=-1, keepdims=True)
            raised = jnp.exp(scores - peak).astype(BF16)
            both = jnp.dot(raised, values[window, 2 * j * pair : 2 * (j + 1) * pair], preferred_element_type=F32)
            ratio = both[:, :pair] / both[:, pair:]
            mixed[at, part] = jnp.where(first, ratio[:chunk], ratio[chunk:]).astype(BF16)

    loads[2].wait()
    block = rows // 2

    @pl.loop(0, rows // block)
    def _(i):
        at = pl.ds(pl.multiple_of(i * block, block), block)
        centre = pl.ds(pl.multiple_of(rim + i * block, cells), block)
        h = hidden[centre, :] + gate1 * jnp.dot(mixed[at, :], w_proj[...], preferred_element_type=F32)
        hidden[centre, :] = h
        normed[at, :] = (normalised(h) * (1.0 + scale2) + shift2).astype(BF16)

    loads[3].wait()
    loads[4].wait()
    ff[...] = jnp.zeros_like(ff)
    slab = width

    @pl.loop(0, w_up.shape[1] // slab)
    def _(c):
        at = pl.ds(pl.multiple_of(c * slab, slab), slab)
        up = jnp.dot(normed[:rows, :], w_up[:, at], preferred_element_type=F32)
        up = jax.nn.gelu(up, approximate=True).astype(BF16)
        ff[...] += jnp.dot(up, w_down[at, :], preferred_element_type=F32)

    loads[5].wait()
    h = hidden[inner, :] + gate2 * ff[...]
    inc[...] = step[...] * jnp.dot(normalised(h).astype(BF16), w_out[...], preferred_element_type=F32)


def scaled_drift(ext, mods, step, bias, weights):
    rim = REACH * GY * GZ
    ext_rows, channels = ext.shape
    rows = ext_rows - 2 * rim
    width = weights[0].shape[1]
    vmem = pl.BlockSpec(memory_space=pltpu.VMEM)
    scratch = [pltpu.VMEM(w.shape, w.dtype) for w in weights] + [
        pltpu.VMEM((ext_rows, width), F32),
        pltpu.VMEM((ext_rows, width), BF16),
        pltpu.VMEM((rows, width), BF16),
        pltpu.VMEM((ext_rows, width), BF16),
        pltpu.VMEM((ext_rows, 2 * width), BF16),
        pltpu.VMEM((rows, width), BF16),
        pltpu.VMEM((rows, width), F32),
        pltpu.SemaphoreType.DMA((len(weights),)),
    ]
    return pl.pallas_call(
        drift_kernel,
        out_shape=jax.ShapeDtypeStruct((rows, channels), F32),
        in_specs=[vmem] * 4 + [pl.BlockSpec(memory_space=pl.ANY)] * len(weights),
        out_specs=vmem,
        scratch_shapes=scratch,
        compiler_params=pltpu.CompilerParams(vmem_limit_bytes=56 * 1024 * 1024),
        cost_estimate=pl.CostEstimate(
            flops=24 * rows * width * width, bytes_accessed=2 * 12 * width * width, transcendentals=0
        ),
        name="drift",
    )(ext, mods, step, bias, *weights)


def local(prev_states, timesteps, step_sizes, slide, w_time, w_ada, w_in, w_qkv, w_proj, w_up, w_down, w_out):
    window, gx = lax.axis_size("win"), lax.axis_size("gx")
    mods = modulation(timesteps[0], w_time, w_ada)
    weights = (w_in, w_qkv[0], w_proj[0], w_up[0], w_down[0], w_out)
    step = jnp.broadcast_to(step_sizes[None, :], (1, prev_states.shape[2]))
    bias = jnp.asarray(pair_bias())
    me = lax.axis_index("win")
    opening, fine = shifted(prev_states[0], slide[0] - 1, window, gx)
    rim = REACH * GY * GZ
    start = jnp.where(me == 0, opening[rim:-rim].astype(F32) + fine.astype(F32), 0.0)
    arrived = [lax.ppermute(start, "win", [(0, t)]) for t in range(2, window, 2)]
    inc = scaled_drift(opening, mods, step, bias, weights)
    inc, arrived = lax.optimization_barrier((inc, arrived))
    even = functools.reduce(jnp.add, arrived, start)
    odd = lax.ppermute(even, "win", [(k, k + 1) for k in range(0, window, 2)])
    for _ in range(SWEEPS - 1):
        ext = scanned(inc, opening, window, gx, False)
        inc = scaled_drift(ext, mods, step, bias, weights)
    inc, odd = lax.optimization_barrier((inc, odd))
    return (scanned(inc, opening, window, gx, True) + (even + odd))[None]


def solution(mesh):
    spread, split, whole = P(("groups", "win"), "gx", None), P(("groups", "win")), P()
    return jax.shard_map(
        local,
        mesh=mesh,
        in_specs=(spread, split, split) + (whole,) * 9,
        out_specs=spread,
        check_vma=False,
    )
```

```python
import functools
import math

import jax
import jax.numpy as jnp
import numpy as np
from jax import lax
from jax.experimental import pallas as pl
from jax.experimental.pallas import tpu as pltpu
from jax.sharding import PartitionSpec as P

HEADS = 12
SWEEPS = 2
GY = 8
GZ = 8
REACH = 3
EPSILON = 1e-06
MESH = pl.DeviceIdType.MESH
F32 = jnp.float32
BF16 = jnp.bfloat16


def project_kernel(active, w_ada, mods):
    mods[...] = jnp.dot(active[...], w_ada[...], preferred_element_type=F32)


def modulation(moment, w_time, w_ada):
    half = w_time.shape[0] // 2
    freqs = jnp.exp(-math.log(10000.0) * jnp.arange(half, dtype=F32) / half)
    angles = moment.astype(F32) * freqs
    embedded = jnp.concatenate([jnp.cos(angles), jnp.sin(angles)])[None, :]
    condition = jax.nn.silu(jnp.dot(embedded.astype(BF16), w_time, preferred_element_type=F32))
    active = jnp.broadcast_to(jax.nn.silu(condition).astype(BF16), (16, w_time.shape[1]))
    width, columns = w_ada.shape[1:]
    return pl.pallas_call(
        project_kernel,
        out_shape=jax.ShapeDtypeStruct((16, columns), F32),
        grid=(columns // width,),
        in_specs=[
            pl.BlockSpec((16, width), lambda i: (0, 0)),
            pl.BlockSpec((width, width), lambda i: (0, i)),
        ],
        out_specs=pl.BlockSpec((16, width), lambda i: (0, i)),
        compiler_params=pltpu.CompilerParams(vmem_limit_bytes=56 * 1024 * 1024),
        name="modulate",
    )(active, w_ada[0])


def pair_bias():
    cells = GY * GZ
    query = np.arange(2 * cells)[:, None]
    key = np.arange((2 * REACH + 2) * cells)[None, :]
    apart_x = key // cells - query // cells
    apart_y = (key % cells // GZ - query % cells // GZ) % GY
    apart_z = (key % GZ - query % GZ) % GZ
    near = (apart_x >= 0) & (apart_x <= 2 * REACH)
    near &= (np.minimum(apart_y, GY - apart_y) <= REACH) & (np.minimum(apart_z, GZ - apart_z) <= REACH)
    bias = np.where(near, 0.0, -1e30).astype(np.float32)
    return np.concatenate([bias, bias], axis=0)


def greet(peers):
    barrier = pltpu.get_barrier_semaphore()
    for peer in peers:
        pl.semaphore_signal(barrier, inc=1, device_id=peer, device_id_type=MESH)
    pl.semaphore_wait(barrier, len(peers))


def swap_rims(ext, send_sem, recv_sem, gx):
    side = lax.axis_index("gx")
    rim = REACH * GY * GZ
    rows = ext.shape[0]
    copies = [
        pltpu.make_async_remote_copy(
            src_ref=ext.at[pl.ds(rows - 2 * rim, rim)],
            dst_ref=ext.at[pl.ds(0, rim)],
            send_sem=send_sem.at[0],
            recv_sem=recv_sem.at[0],
            device_id={"gx": lax.rem(side + 1, gx)},
            device_id_type=MESH,
        ),
        pltpu.make_async_remote_copy(
            src_ref=ext.at[pl.ds(rim, rim)],
            dst_ref=ext.at[pl.ds(rows - rim, rim)],
            send_sem=send_sem.at[1],
            recv_sem=recv_sem.at[1],
            device_id={"gx": lax.rem(side + gx - 1, gx)},
            device_id_type=MESH,
        ),
    ]
    for copy in copies:
        copy.start()
    for copy in copies:
        copy.wait()


def shift_kernel(
    offset, window, gx, prev, ext, fine, own, own_fine, send_sem, recv_sem, fine_send, fine_recv, rim_send, rim_recv
):
    me, side = lax.axis_index("win"), lax.axis_index("gx")
    rows = prev.shape[0]
    rim = REACH * GY * GZ
    own[...] = prev[...].astype(BF16)
    own_fine[...] = (prev[...] - own[...].astype(F32)).astype(BF16)
    peers = [{"gx": lax.rem(side + 1, gx)}]
    peers += [{"win": lax.rem(me + d, window)} for d in range(1, window)] if offset else []
    greet(peers)

    def copy_to(target, slot):
        return pltpu.make_async_remote_copy(
            src_ref=own,
            dst_ref=ext.at[pl.ds(rim, rows)],
            send_sem=send_sem.at[slot],
            recv_sem=recv_sem,
            device_id={"win": target},
            device_id_type=MESH,
        )

    last = window - 1
    fine_copy = pltpu.make_async_remote_copy(
        src_ref=own_fine,
        dst_ref=fine,
        send_sem=fine_send,
        recv_sem=fine_recv,
        device_id={"win": 0},
        device_id_type=MESH,
    )

    @pl.when(me > 0)
    def _():
        fine[...] = jnp.zeros_like(fine)

    if offset:

        @pl.when(me == last)
        def _():
            for t in range(last - offset, last):
                copy_to(t, t).start()

        if offset < last:

            @pl.when((me < last) & (me >= offset))
            def _():
                copy_to(me - offset, last).start()

        @pl.when(me == offset)
        def _():
            fine_copy.start()

        @pl.when(me == last)
        def _():
            ext[pl.ds(rim, rows), :] = own[...]

        @pl.when(me < last)
        def _():
            copy_to(me, 0).wait_recv()

    else:
        ext[pl.ds(rim, rows), :] = own[...]

        @pl.when(me == 0)
        def _():
            fine[...] = own_fine[...]

    swap_rims(ext, rim_send, rim_recv, gx)
    if offset:

        @pl.when(me == last)
        def _():
            for t in range(last - offset, last):
                copy_to(t, t).wait_send()

        if offset < last:

            @pl.when((me < last) & (me >= offset))
            def _():
                copy_to(me - offset, last).wait_send()

        @pl.when(me == offset)
        def _():
            fine_copy.wait_send()

        @pl.when(me == 0)
        def _():
            fine_copy.wait_recv()


def shifted(prev, offset, window, gx):
    rows, channels = prev.shape
    ext_rows = rows + 2 * REACH * GY * GZ

    def branch(static):
        def call(x):
            return pl.pallas_call(
                functools.partial(shift_kernel, static, window, gx),
                out_shape=[
                    jax.ShapeDtypeStruct((ext_rows, channels), BF16),
                    jax.ShapeDtypeStruct((rows, channels), BF16),
                ],
                in_specs=[pl.BlockSpec(memory_space=pltpu.VMEM)],
                out_specs=[pl.BlockSpec(memory_space=pltpu.VMEM)] * 2,
                scratch_shapes=[
                    pltpu.VMEM((rows, channels), BF16),
                    pltpu.VMEM((rows, channels), BF16),
                    pltpu.SemaphoreType.DMA((window,)),
                    pltpu.SemaphoreType.DMA,
                    pltpu.SemaphoreType.DMA,
                    pltpu.SemaphoreType.DMA,
                    pltpu.SemaphoreType.DMA((2,)),
                    pltpu.SemaphoreType.DMA((2,)),
                ],
                compiler_params=pltpu.CompilerParams(collective_id=2 + static, has_side_effects=True),
                name=f"shift_{static}",
            )(x)

        return call

    return lax.switch(offset, [branch(static) for static in range(window)], prev)


def scan_kernel(
    final, window, gx, inc, ext_in, fine, out,
    contrib, partner, half_sum, slots, fine_sum, fine_slot, half_before, back_from, back_into, before,
    pair_send, pair_recv, far_send, far_recv, fine_send, fine_recv, back_send, back_recv, rim_send, rim_recv,
):
    me, side = lax.axis_index("win"), lax.axis_index("gx")
    rows = inc.shape[0]
    half = rows // 2
    rim = REACH * GY * GZ
    groups = window // 2
    z, y = me // 2, lax.rem(me, 2)
    mate = {"win": me + 1 - 2 * y}

    opening = jnp.where(me == 0, ext_in[pl.ds(rim, rows), :].astype(F32) + fine[...].astype(F32), 0.0)
    contrib[...] = (inc[...] + opening).astype(contrib.dtype)
    peers = [mate]
    peers += [{"win": lax.rem(me + 2 * d, window)} for d in range(1, groups)]
    if not final:
        peers.append({"gx": lax.rem(side + 1, gx)})
    greet(peers)

    def pair_copy(part):
        return pltpu.make_async_remote_copy(
            src_ref=contrib.at[pl.ds(part * half, half)],
            dst_ref=partner.at[pl.ds(part * half, half)],
            send_sem=pair_send.at[part],
            recv_sem=pair_recv.at[part],
            device_id=mate,
            device_id_type=MESH,
        )

    def far_copy(target, slot):
        return pltpu.make_async_remote_copy(
            src_ref=half_sum,
            dst_ref=slots.at[slot],
            send_sem=far_send.at[target],
            recv_sem=far_recv.at[slot],
            device_id={"win": target * 2 + y},
            device_id_type=MESH,
        )

    def fine_copy(target):
        return pltpu.make_async_remote_copy(
            src_ref=fine_sum,
            dst_ref=fine_slot,
            send_sem=fine_send.at[target],
            recv_sem=fine_recv,
            device_id={"win": target * 2 + y},
            device_id_type=MESH,
        )

    back_copy = pltpu.make_async_remote_copy(
        src_ref=back_from,
        dst_ref=back_into,
        send_sem=back_send,
        recv_sem=back_recv,
        device_id=mate,
        device_id_type=MESH,
    )

    @pl.when(y == 0)
    def _():
        pair_copy(1).start()
        pair_copy(0).start()
        pair_copy(0).wait_recv()
        share = contrib[:half, :].astype(F32) + partner[:half, :].astype(F32)
        half_sum[...] = share.astype(BF16)
        fine_sum[...] = (share - share.astype(BF16).astype(F32)).astype(BF16)

    @pl.when(y == 1)
    def _():
        pair_copy(0).start()
        pair_copy(1).wait_recv()
        share = contrib[half:, :].astype(F32) + partner[half:, :].astype(F32)
        half_sum[...] = share.astype(BF16)
        fine_sum[...] = (share - share.astype(BF16).astype(F32)).astype(BF16)

    for target in range(1, groups):
        for source in range(target):

            @pl.when(z == source)
            def _():
                far_copy(target, source).start()
                if final and source == 0:
                    fine_copy(target).start()

    half_before[...] = jnp.zeros_like(half_before)
    for source in range(groups - 1):

        @pl.when(z > source)
        def _():
            far_copy(source + 1, source).wait_recv()
            half_before[...] += slots[source].astype(F32)
            if final and source == 0:
                fine_copy(1).wait_recv()
                half_before[...] += fine_slot[...].astype(F32)

    before[...] = jnp.zeros_like(before)

    @pl.when(z > 0)
    def _():
        back_from[...] = half_before[...].astype(back_from.dtype)
        back_copy.start()
        back_copy.wait_recv()

    @pl.when((z > 0) & (y == 0))
    def _():
        before[:half, :] = half_before[...]
        before[half:, :] = back_into[...].astype(F32)

    @pl.when((z > 0) & (y == 1))
    def _():
        before[:half, :] = back_into[...].astype(F32)
        before[half:, :] = half_before[...]

    @pl.when(y == 1)
    def _():
        pair_copy(0).wait_recv()
        before[...] += partner[...].astype(F32)

    if final:
        out[...] = before[...] + (inc[...] + opening)
    else:
        out[pl.ds(rim, rows), :] = jnp.where(me == 0, opening, before[...]).astype(BF16)
        swap_rims(out, rim_send, rim_recv, gx)

    pair_copy(0).wait_send()

    @pl.when(y == 0)
    def _():
        pair_copy(1).wait_send()

    for target in range(1, groups):

        @pl.when(z < target)
        def _():
            far_copy(target, 0).wait_send()

        if final:

            @pl.when(z == 0)
            def _():
                fine_copy(target).wait_send()

    @pl.when(z > 0)
    def _():
        back_copy.wait_send()


def scanned(inc, ext, fine, window, gx, final):
    kind = F32 if final else BF16
    rows, channels = inc.shape
    half, groups = rows // 2, window // 2
    return pl.pallas_call(
        functools.partial(scan_kernel, final, window, gx),
        out_shape=jax.ShapeDtypeStruct(inc.shape, F32) if final else jax.ShapeDtypeStruct(ext.shape, BF16),
        in_specs=[pl.BlockSpec(memory_space=pltpu.VMEM)] * 3,
        out_specs=pl.BlockSpec(memory_space=pltpu.VMEM),
        scratch_shapes=[
            pltpu.VMEM((rows, channels), kind),
            pltpu.VMEM((rows, channels), kind),
            pltpu.VMEM((half, channels), BF16),
            pltpu.VMEM((groups, half, channels), BF16),
            pltpu.VMEM((half, channels), BF16),
            pltpu.VMEM((half, channels), BF16),
            pltpu.VMEM((half, channels), F32),
            pltpu.VMEM((half, channels), kind),
            pltpu.VMEM((half, channels), kind),
            pltpu.VMEM((rows, channels), F32),
            pltpu.SemaphoreType.DMA((2,)),
            pltpu.SemaphoreType.DMA((2,)),
            pltpu.SemaphoreType.DMA((groups,)),
            pltpu.SemaphoreType.DMA((groups,)),
            pltpu.SemaphoreType.DMA((groups,)),
            pltpu.SemaphoreType.DMA,
            pltpu.SemaphoreType.DMA,
            pltpu.SemaphoreType.DMA,
            pltpu.SemaphoreType.DMA((2,)),
            pltpu.SemaphoreType.DMA((2,)),
        ],
        compiler_params=pltpu.CompilerParams(collective_id=int(final), has_side_effects=True),
        name="scan_final" if final else "scan_next",
    )(inc, ext, fine)


def normalised(values):
    centred = values - jnp.mean(values, axis=-1, keepdims=True)
    spread = jnp.mean(centred * centred, axis=-1, keepdims=True)
    return centred * lax.rsqrt(spread + EPSILON)


def drift_kernel(
    ext, mods, step, bias, w_in_hbm, w_qkv_hbm, w_proj_hbm, w_up_hbm, w_down_hbm, w_out_hbm, inc,
    w_in, w_qkv, w_proj, w_up, w_down, w_out, hidden, normed, queries, keys, values, mixed, ff, sems,
):
    cells = GY * GZ
    rim = REACH * cells
    ext_rows = ext.shape[0]
    rows = inc.shape[0]
    width = hidden.shape[1]
    pair = 2 * width // HEADS
    pairs = HEADS // 2
    loads = [
        pltpu.make_async_copy(source, target, sems.at[i])
        for i, (source, target) in enumerate(
            [
                (w_in_hbm, w_in),
                (w_qkv_hbm, w_qkv),
                (w_proj_hbm, w_proj),
                (w_up_hbm, w_up),
                (w_down_hbm, w_down),
                (w_out_hbm, w_out),
            ]
        )
    ]
    for load in loads:
        load.start()
    shift1, scale1, gate1, shift2, scale2, gate2 = [mods[0:1, i * width : (i + 1) * width] for i in range(6)]

    loads[0].wait()
    chunk = 2 * cells

    @pl.loop(0, ext_rows // chunk)
    def _(i):
        at = pl.ds(pl.multiple_of(i * chunk, chunk), chunk)
        h = jnp.dot(ext[at, :], w_in[...], preferred_element_type=F32)
        hidden[at, :] = h
        normed[at, :] = (normalised(h) * (1.0 + scale1) + shift1).astype(BF16)
        values[at, :] = jnp.ones((chunk, 2 * width), BF16)

    loads[1].wait()
    inner = pl.ds(rim, rows)
    for j in range(pairs):
        part = slice(j * pair, (j + 1) * pair)
        queries[:, part] = (
            jnp.dot(normed[inner, :], w_qkv[:, part], preferred_element_type=F32) * (pair // 2) ** -0.5
        ).astype(BF16)
        keys[:, part] = jnp.dot(
            normed[...], w_qkv[:, width + j * pair : width + (j + 1) * pair], preferred_element_type=F32
        ).astype(BF16)
        values[:, 2 * j * pair : (2 * j + 1) * pair] = jnp.dot(
            normed[...], w_qkv[:, 2 * width + j * pair : 2 * width + (j + 1) * pair], preferred_element_type=F32
        ).astype(BF16)

    first = lax.broadcasted_iota(jnp.int32, (chunk, pair), 1) < pair // 2
    span = chunk + 2 * rim

    @pl.loop(0, rows // chunk)
    def _(i):
        at = pl.ds(pl.multiple_of(i * chunk, chunk), chunk)
        window = pl.ds(pl.multiple_of(i * chunk, chunk), span)
        for j in range(pairs):
            part = slice(j * pair, (j + 1) * pair)
            q = queries[at, part]
            zero = jnp.zeros_like(q)
            stacked = jnp.concatenate([jnp.where(first, q, zero), jnp.where(first, zero, q)], axis=0)
            scores = lax.dot_general(
                stacked, keys[window, part], (((1,), (1,)), ((), ())), preferred_element_type=F32
            )
            scores = scores + bias[...]
            peak = jnp.max(scores, axis=-1, keepdims=True)
            raised = jnp.exp(scores - peak).astype(BF16)
            both = jnp.dot(raised, values[window, 2 * j * pair : 2 * (j + 1) * pair], preferred_element_type=F32)
            ratio = both[:, :pair] / both[:, pair:]
            mixed[at, part] = jnp.where(first, ratio[:chunk], ratio[chunk:]).astype(BF16)

    loads[2].wait()
    block = rows // 2

    @pl.loop(0, rows // block)
    def _(i):
        at = pl.ds(pl.multiple_of(i * block, block), block)
        centre = pl.ds(pl.multiple_of(rim + i * block, cells), block)
        h = hidden[centre, :] + gate1 * jnp.dot(mixed[at, :], w_proj[...], preferred_element_type=F32)
        hidden[centre, :] = h
        normed[at, :] = (normalised(h) * (1.0 + scale2) + shift2).astype(BF16)

    loads[3].wait()
    loads[4].wait()
    ff[...] = jnp.zeros_like(ff)
    slab = width

    @pl.loop(0, w_up.shape[1] // slab)
    def _(c):
        at = pl.ds(pl.multiple_of(c * slab, slab), slab)
        up = jnp.dot(normed[:rows, :], w_up[:, at], preferred_element_type=F32)
        up = jax.nn.gelu(up, approximate=True).astype(BF16)
        ff[...] += jnp.dot(up, w_down[at, :], preferred_element_type=F32)

    loads[5].wait()
    h = hidden[inner, :] + gate2 * ff[...]
    inc[...] = step[...] * jnp.dot(normalised(h).astype(BF16), w_out[...], preferred_element_type=F32)


def scaled_drift(ext, mods, step, bias, weights):
    rim = REACH * GY * GZ
    ext_rows, channels = ext.shape
    rows = ext_rows - 2 * rim
    width = weights[0].shape[1]
    vmem = pl.BlockSpec(memory_space=pltpu.VMEM)
    scratch = [pltpu.VMEM(w.shape, w.dtype) for w in weights] + [
        pltpu.VMEM((ext_rows, width), F32),
        pltpu.VMEM((ext_rows, width), BF16),
        pltpu.VMEM((rows, width), BF16),
        pltpu.VMEM((ext_rows, width), BF16),
        pltpu.VMEM((ext_rows, 2 * width), BF16),
        pltpu.VMEM((rows, width), BF16),
        pltpu.VMEM((rows, width), F32),
        pltpu.SemaphoreType.DMA((len(weights),)),
    ]
    return pl.pallas_call(
        drift_kernel,
        out_shape=jax.ShapeDtypeStruct((rows, channels), F32),
        in_specs=[vmem] * 4 + [pl.BlockSpec(memory_space=pl.ANY)] * len(weights),
        out_specs=vmem,
        scratch_shapes=scratch,
        compiler_params=pltpu.CompilerParams(vmem_limit_bytes=56 * 1024 * 1024),
        name="drift",
    )(ext, mods, step, bias, *weights)


def local(prev_states, timesteps, step_sizes, slide, w_time, w_ada, w_in, w_qkv, w_proj, w_up, w_down, w_out):
    window, gx = lax.axis_size("win"), lax.axis_size("gx")
    mods = modulation(timesteps[0], w_time, w_ada)
    weights = (w_in, w_qkv[0], w_proj[0], w_up[0], w_down[0], w_out)
    step = jnp.broadcast_to(step_sizes[None, :], (1, prev_states.shape[2]))
    bias = jnp.asarray(pair_bias())
    opening, fine = shifted(prev_states[0], slide[0] - 1, window, gx)
    ext = opening
    for sweep in range(SWEEPS):
        inc = scaled_drift(ext, mods, step, bias, weights)
        ext = scanned(inc, opening, fine, window, gx, sweep == SWEEPS - 1)
    return ext[None]


def solution(mesh):
    spread, split, whole = P(("groups", "win"), "gx", None), P(("groups", "win")), P()
    return jax.shard_map(
        local,
        mesh=mesh,
        in_specs=(spread, split, split) + (whole,) * 9,
        out_specs=spread,
        check_vma=False,
    )
```
